1024 devices in a mesh: blk: 256 (over y_lo, x, z, core), aux: 4 (over y_hi).
Axes of the slice: x: 4, y: 8 (y_hi: 4, y_lo: 2; y = y_hi * 2 + y_lo), z: 16, core: 2. Of those that a mesh axis runs over, the one named last changes fastest.
Arguments:
- factor: bfloat16 [2048, 16, 704], P(('blk', 'aux')), may hold values from -0.125 to 0.125
- amplitude_forward: bfloat16 [256, 3072, 1024], P('blk', 'aux'), may hold values from -6 to 6
- amplitude_reversed: bfloat16 [256, 3072, 1024], P('blk', 'aux'), may hold values from -6 to 6
- block_map: int32 [256, 2], P('blk'), may hold values from 0 to 21, as said below
- pair_list: int32 [3072, 2], P('aux'), may hold values from 0 to 63, as said below
- virt_energy: float32 [16], replicated, may hold values from 0.5 to 3
- occ_energy: float32 [64], replicated, may hold values from -3 to -0.5
Outputs:
- update: float32 [4, 196608], P('aux', 'blk')
The draws below stay inside these ranges and needn't reach their ends.
Inputs may be any that keep to these rules, and one draw needn't show every extreme that they name: `block_map`: each row holds two different block numbers below 22; no two rows are equal. `pair_list`: no two rows are equal.
All inputs are finite; a program needn't handle non-finite values.
Results may differ from the reference program's by a relative error of at most 0.0029.
Values may be sent and summed in bfloat16 or wider, within the bound.
No kernel may reach another device: no remote copies, remote signals or barrier semaphores. Data moves between devices by JAX's collectives and lax.ppermute only.
A program may use at most 64 MiB of HBM per device.

```python
import jax
import jax.numpy as jnp
from jax import lax

NV = 704
NO = 64
NAUX = 2048
AW = 16
BLOCK_VIRTUALS = 32
PAIR_DEV = 768
NB = 22
SLOT_COUNT = 256
OCCUPIED_PAIRS = 3072
N_AUX = 4


def draw_block_map(key, part):
    key = jax.random.fold_in(key, 11)
    count_of_pairs = NB * (NB - 1)
    selected_entry = jax.random.permutation(jax.random.fold_in(key, 1), count_of_pairs - 2)[:SLOT_COUNT - 2] + 1
    encoded_listing = jnp.concatenate([jnp.array([0, count_of_pairs - 1], jnp.int32), selected_entry.astype(jnp.int32)])
    encoded_listing = encoded_listing[jax.random.permutation(jax.random.fold_in(key, 2), SLOT_COUNT)]
    leading = encoded_listing // (NB - 1)
    remainder = encoded_listing % (NB - 1)
    trailing = remainder + (remainder >= leading).astype(jnp.int32)
    return jnp.stack([leading, trailing], axis=1).astype(jnp.int32)


def draw_pair_list(key, part):
    key = jax.random.fold_in(key, 23)
    count_of_pairs = NO * NO
    selected_entry = jax.random.permutation(jax.random.fold_in(key, 1), count_of_pairs - 2)[:OCCUPIED_PAIRS - 2] + 1
    encoded_listing = jnp.concatenate([jnp.array([0, count_of_pairs - 1], jnp.int32), selected_entry.astype(jnp.int32)])
    encoded_listing = encoded_listing[jax.random.permutation(jax.random.fold_in(key, 2), OCCUPIED_PAIRS)]
    return jnp.stack([encoded_listing // NO, encoded_listing % NO], axis=1).astype(jnp.int32)


def raised(entries, key, source, target, blocks, factor):
    def block_of(position):
        return (jnp.arange(entries.shape[position]) // (entries.shape[position] // blocks)).reshape((-1,) + (1,) * (entries.ndim - 1 - position))

    near = jax.random.permutation(key, blocks)[block_of(target)]
    second = (block_of(target) + blocks // 2) % blocks
    return jnp.where((block_of(source) == near) | (block_of(source) == second), factor * entries, entries)


def block_scale(rng, dims, cuts, low, top_value):
    gain, own = 1.0, jax.random.fold_in(rng, 6)
    for axis_at, parts in cuts:
        steps = jnp.exp(jax.random.uniform(jax.random.fold_in(own, axis_at), (parts,), jnp.float32, low / len(cuts), top_value / len(cuts)))
        gain = gain * jnp.repeat(steps, dims[axis_at] // parts).reshape([-1 if axis == axis_at else 1 for axis in range(len(dims))])
    return gain


def centred(key, shape, width, reach, cuts=(), dtype=jnp.bfloat16):
    entries = width * jax.random.normal(key, shape, jnp.float32)
    if cuts:
        entries = entries * block_scale(key, shape, cuts, -0.22, 0.18)
    return jnp.clip(entries, -reach, reach).astype(dtype)


def noise_with(rng, shape, scale, most, pieces, heavy, held_as=jnp.bfloat16):
    result = scale * jax.random.normal(rng, shape, jnp.float32)
    if pieces:
        result = result * block_scale(rng, shape, pieces, -0.22, 0.18)
    return jnp.clip(raised(result, jax.random.fold_in(rng, 3), *heavy), -most, most).astype(held_as)


def setup_inputs(seed: int = 0) -> dict:
    key_list = jax.random.split(jax.random.key(seed), 8)
    return {
        "factor": centred(key_list[0], (NAUX, AW, NV), NAUX ** -0.5, 0.125, ((0, 1024),)),
        "amplitude_forward": noise_with(key_list[1], (SLOT_COUNT, OCCUPIED_PAIRS, BLOCK_VIRTUALS * BLOCK_VIRTUALS), 0.25, 6.0, ((0, 256), (1, 4)), (0, 1, 256, 6.0)),
        "amplitude_reversed": noise_with(key_list[2], (SLOT_COUNT, OCCUPIED_PAIRS, BLOCK_VIRTUALS * BLOCK_VIRTUALS), 0.25, 6.0, ((0, 256), (1, 4)), (0, 1, 256, 6.0)),
        "block_map": draw_block_map(jax.random.fold_in(key_list[7], 71), 0),
        "pair_list": draw_pair_list(jax.random.fold_in(key_list[7], 71), 0),
        "virt_energy": jnp.clip(jax.random.uniform(key_list[5], (AW,), jnp.float32, 0.5, 3.0), 0.5, 3.0),
        "occ_energy": jnp.clip(jax.random.uniform(key_list[6], (NO,), jnp.float32, -3.0, -0.5), -3.0, -0.5),
    }


def reference(factor, amplitude_forward, amplitude_reversed, block_map, pair_list, virt_energy, occ_energy):
    aux_rows = factor.shape[0]

    def slot_step(running, slot_data):
        direct, mirror, block_pair = slot_data
        left_slab = lax.dynamic_slice_in_dim(factor, (block_pair[0] * BLOCK_VIRTUALS).astype(jnp.int32), BLOCK_VIRTUALS, 2).reshape(aux_rows, AW * BLOCK_VIRTUALS)
        right_slab = lax.dynamic_slice_in_dim(factor, (block_pair[1] * BLOCK_VIRTUALS).astype(jnp.int32), BLOCK_VIRTUALS, 2).reshape(aux_rows, AW * BLOCK_VIRTUALS)
        coulomb = lax.dot_general(left_slab, right_slab, (((0,), (0,)), ((), ())), preferred_element_type=jnp.float32)
        weights = coulomb.reshape(AW, BLOCK_VIRTUALS, AW, BLOCK_VIRTUALS).transpose(0, 2, 1, 3).reshape(AW * AW, BLOCK_VIRTUALS * BLOCK_VIRTUALS).astype(jnp.bfloat16)
        direct_term = lax.dot_general(direct, weights, (((1,), (1,)), ((), ())), preferred_element_type=jnp.float32)
        swapped = lax.dot_general(mirror, weights, (((1,), (1,)), ((), ())), preferred_element_type=jnp.float32)
        swapped = swapped.reshape(-1, AW, AW).transpose(0, 2, 1).reshape(-1, AW * AW)
        return running + direct_term + swapped, None

    start_sum = jnp.zeros((OCCUPIED_PAIRS, AW * AW), jnp.float32)
    residual, _ = lax.scan(slot_step, start_sum, (amplitude_forward, amplitude_reversed, block_map))
    pair_energy = occ_energy[pair_list[:, 0]] + occ_energy[pair_list[:, 1]]
    denominator = (pair_energy[:, None, None] - virt_energy[None, :, None]) - virt_energy[None, None, :]
    update = residual / denominator.reshape(OCCUPIED_PAIRS, AW * AW)
    return update.reshape(N_AUX, PAIR_DEV * AW * AW)
```

```python
import jax
import jax.numpy as jnp
from jax import lax
from jax.sharding import Mesh
from jax.sharding import PartitionSpec as P

AW = 16
BLOCK_VIRTUALS = 32
NV = 704
BLK = ("yl", "x", "z", "core")
PLANE = ("yl", "x", "core")


def table_lookup(index_list, table):
    slots_here = jnp.arange(table.shape[0], dtype=jnp.int32)
    return jnp.sum(
        jnp.where(index_list[:, None] == slots_here[None, :], table[None, :], 0.0), axis=1
    )


def one_hot_rows(columns, width):
    cols = lax.broadcasted_iota(jnp.int32, (columns.shape[0], width), 1)
    return (columns[:, None] == cols).astype(jnp.bfloat16)


def select_rows(hot, rows):
    return lax.dot_general(
        hot, rows, (((1,), (1,)), ((), ())), preferred_element_type=jnp.float32
    ).astype(jnp.bfloat16)


def shards(
    factor, amplitude_forward, amplitude_reversed, block_map, pair_list, virt_energy, occ_energy
):
    plane_map = lax.all_gather(block_map, PLANE, axis=0, tiled=True)
    line = lax.all_gather(factor, "z", axis=0, tiled=True)
    q_line = line.shape[0]
    wanted = (
        plane_map.reshape(-1, 1) * BLOCK_VIRTUALS + jnp.arange(BLOCK_VIRTUALS, dtype=jnp.int32)
    ).reshape(-1)
    line = line.transpose(1, 0, 2).reshape(AW * q_line, NV)
    picked = select_rows(one_hot_rows(wanted, NV), line)
    picked = picked.reshape(16, 2 * BLOCK_VIRTUALS, AW * q_line)
    picked = lax.all_to_all(picked, PLANE, 0, 0, tiled=True)
    picked = picked.reshape(16, 2, BLOCK_VIRTUALS, AW, q_line)
    partial_sum = jnp.einsum(
        "scaq,sdbq->acbd", picked[:, 0], picked[:, 1], preferred_element_type=jnp.float32
    )
    partial_sum = partial_sum.reshape(4, 4 * BLOCK_VIRTUALS, AW * BLOCK_VIRTUALS)
    quarters = lax.all_to_all(partial_sum, "yh", 0, 0, tiled=True)
    coulomb = quarters[0] + quarters[1] + quarters[2] + quarters[3]
    weights = (
        coulomb.astype(jnp.bfloat16)
        .reshape(4, BLOCK_VIRTUALS, AW, BLOCK_VIRTUALS)
        .transpose(0, 2, 1, 3)
        .reshape(4 * AW, BLOCK_VIRTUALS * BLOCK_VIRTUALS)
    )
    weights = lax.all_gather(weights, "yh", axis=0, tiled=True)
    mirrored = (
        weights.reshape(AW, AW, -1).transpose(1, 0, 2).reshape(AW * AW, -1)
    )
    direct_term = lax.dot_general(
        amplitude_forward[0], weights, (((1,), (1,)), ((), ())), preferred_element_type=jnp.float32
    )
    swapped = lax.dot_general(
        amplitude_reversed[0], mirrored, (((1,), (1,)), ((), ())), preferred_element_type=jnp.float32
    )
    slot_term = (direct_term + swapped).astype(jnp.bfloat16)
    row = jnp.arange(768, dtype=jnp.int32)
    source = jnp.arange(768, dtype=jnp.int32).reshape(8, 16, 2, 3).transpose(0, 2, 1, 3).reshape(-1)
    hot = one_hot_rows(source, 768)
    ordered = lax.dot_general(
        hot, slot_term, (((1,), (0,)), ((), ())), preferred_element_type=jnp.float32
    ).astype(jnp.bfloat16)
    ordered = lax.all_to_all(ordered.reshape(16, 48, 256), PLANE, 0, 0, tiled=True)
    plane_sum = jnp.sum(ordered.astype(jnp.float32), axis=0).reshape(16, 768)
    owned = jnp.sum(lax.all_to_all(plane_sum, "z", 0, 0, tiled=True), axis=0)

    owned_len = owned.shape[0]
    offset = lax.axis_index(BLK) * owned_len
    flat_index = offset + jnp.arange(owned_len, dtype=jnp.int32)
    pair_at = flat_index // (AW * AW)
    cell_index = flat_index % (AW * AW)
    pair_energy = table_lookup(pair_list[:, 0], occ_energy) + table_lookup(
        pair_list[:, 1], occ_energy
    )
    owned_pair = table_lookup(pair_at, pair_energy)
    energy_a = table_lookup(cell_index // AW, virt_energy)
    energy_b = table_lookup(cell_index % AW, virt_energy)
    denominator = owned_pair - energy_a - energy_b
    return (owned / denominator).reshape(1, owned_len)


def solution(mesh):
    fine = Mesh(mesh.devices.reshape(2, 4, 16, 2, 4), BLK + ("yh",))
    placed = (
        P(BLK + ("yh",), None, None),
        P(BLK, "yh", None),
        P(BLK, "yh", None),
        P(BLK, None),
        P("yh", None),
        P(),
        P(),
    )
    return jax.shard_map(
        shards, mesh=fine, in_specs=placed, out_specs=P("yh", BLK), check_vma=False
    )
```

```python
import jax
import jax.numpy as jnp
from jax import lax
from jax.experimental import pallas as pl
from jax.experimental.pallas import tpu as pltpu
from jax.sharding import Mesh
from jax.sharding import PartitionSpec as P

AW = 16
BLOCK_VIRTUALS = 32
NV = 704
BLK = ("yl", "x", "z", "core")
PLANE = ("yl", "x", "core")
GROUP = 4
LANES = 128


def swap_lane_blocks(tiles):
    lane = lax.broadcasted_iota(jnp.int32, tiles[0].shape, 1)
    block = lax.shift_right_logical(lane, 5)
    result = []
    for j in range(GROUP):
        out = None
        for i in range(GROUP):
            shift = (i - j) * BLOCK_VIRTUALS % LANES
            moved = pltpu.roll(tiles[i], shift, 1) if shift else tiles[i]
            out = moved if out is None else jnp.where(block == i, moved, out)
        result.append(out)
    return result


def integrals_kernel(picked_ref, out_ref, left_ref, right_ref, product_ref):
    for source in range(0, 16, GROUP):
        for first in range(0, AW, GROUP):
            lanes = slice(first * BLOCK_VIRTUALS, first * BLOCK_VIRTUALS + LANES)
            tiles = [
                picked_ref[source + i, :, lanes].astype(jnp.float32) for i in range(GROUP)
            ]
            depth = slice(source * BLOCK_VIRTUALS, source * BLOCK_VIRTUALS + LANES)
            for j, tile in enumerate(swap_lane_blocks(tiles)):
                rows = slice((first + j) * BLOCK_VIRTUALS, (first + j + 1) * BLOCK_VIRTUALS)
                tile = tile.astype(jnp.bfloat16)
                left_ref[rows, depth] = tile[:BLOCK_VIRTUALS]
                right_ref[rows, depth] = tile[BLOCK_VIRTUALS:]
    product_ref[...] = lax.dot_general(
        left_ref[...],
        right_ref[...],
        (((1,), (1,)), ((), ())),
        preferred_element_type=jnp.float32,
    ).reshape(product_ref.shape)
    for c in range(0, BLOCK_VIRTUALS, GROUP):
        for b in range(0, AW, GROUP):
            lanes = slice(b * BLOCK_VIRTUALS, b * BLOCK_VIRTUALS + LANES)
            tiles = [product_ref[:, c + i, lanes] for i in range(GROUP)]
            for j, tile in enumerate(swap_lane_blocks(tiles)):
                out_ref[b + j, :, c * BLOCK_VIRTUALS : c * BLOCK_VIRTUALS + LANES] = tile


def block_integrals(picked):
    side = AW * BLOCK_VIRTUALS
    return pl.pallas_call(
        integrals_kernel,
        out_shape=jax.ShapeDtypeStruct((AW, AW, BLOCK_VIRTUALS**2), jnp.float32),
        in_specs=[pl.BlockSpec(memory_space=pltpu.VMEM)],
        out_specs=pl.BlockSpec(memory_space=pltpu.VMEM),
        scratch_shapes=[
            pltpu.VMEM((side, side), jnp.bfloat16),
            pltpu.VMEM((side, side), jnp.bfloat16),
            pltpu.VMEM((AW, BLOCK_VIRTUALS, side), jnp.float32),
        ],
        compiler_params=pltpu.CompilerParams(vmem_limit_bytes=24 * 1024 * 1024),
        cost_estimate=pl.CostEstimate(
            flops=2 * side**3, bytes_accessed=2 * 1024 * 1024, transcendentals=0
        ),
        name="block_integrals",
    )(picked)


def table_lookup(index_list, table):
    slots_here = jnp.arange(table.shape[0], dtype=jnp.int32)
    return jnp.sum(
        jnp.where(index_list[:, None] == slots_here[None, :], table[None, :], 0.0), axis=1
    )


def one_hot_rows(columns, width):
    cols = lax.broadcasted_iota(jnp.int32, (columns.shape[0], width), 1)
    return (columns[:, None] == cols).astype(jnp.bfloat16)


def select_rows(hot, rows):
    return lax.dot_general(
        hot, rows, (((1,), (1,)), ((), ())), preferred_element_type=jnp.float32
    ).astype(jnp.bfloat16)


def shards(
    factor, amplitude_forward, amplitude_reversed, block_map, pair_list, virt_energy, occ_energy
):
    plane_map = lax.all_to_all(
        jnp.broadcast_to(block_map, (16, 2)), PLANE, 0, 0, tiled=True
    )
    line = lax.all_gather(factor, "z", axis=0, tiled=True)
    q_line = line.shape[0]
    wanted = (
        plane_map.reshape(-1, 1) * BLOCK_VIRTUALS + jnp.arange(BLOCK_VIRTUALS, dtype=jnp.int32)
    ).reshape(-1)
    line = line.transpose(1, 0, 2).reshape(AW * q_line, NV)
    picked = select_rows(one_hot_rows(wanted, NV), line)
    picked = picked.reshape(16, 2 * BLOCK_VIRTUALS, AW * q_line)
    picked = lax.all_to_all(picked, PLANE, 0, 0, tiled=True)
    partial_sum = block_integrals(picked).reshape(4, 4 * AW, -1)
    quarters = lax.all_to_all(partial_sum, "yh", 0, 0, tiled=True)
    coulomb = quarters[0] + quarters[1] + quarters[2] + quarters[3]
    mirrored = lax.all_gather(coulomb.astype(jnp.bfloat16), "yh", axis=0, tiled=True)
    weights = mirrored.reshape(AW, AW, -1).transpose(1, 0, 2).reshape(AW * AW, -1)
    direct_term = lax.dot_general(
        amplitude_forward[0], weights, (((1,), (1,)), ((), ())), preferred_element_type=jnp.float32
    )
    swapped = lax.dot_general(
        amplitude_reversed[0], mirrored, (((1,), (1,)), ((), ())), preferred_element_type=jnp.float32
    )
    slot_term = (direct_term + swapped).astype(jnp.bfloat16)
    row = jnp.arange(768, dtype=jnp.int32)
    source = jnp.arange(768, dtype=jnp.int32).reshape(8, 16, 2, 3).transpose(0, 2, 1, 3).reshape(-1)
    hot = one_hot_rows(source, 768)
    ordered = lax.dot_general(
        hot, slot_term, (((1,), (0,)), ((), ())), preferred_element_type=jnp.float32
    ).astype(jnp.bfloat16)
    ordered = lax.all_to_all(ordered.reshape(16, 48, 256), PLANE, 0, 0, tiled=True)
    plane_sum = jnp.sum(ordered.astype(jnp.float32), axis=0).reshape(16, 768)
    owned = jnp.sum(lax.all_to_all(plane_sum, "z", 0, 0, tiled=True), axis=0)

    owned_len = owned.shape[0]
    offset = lax.axis_index(BLK) * owned_len
    flat_index = offset + jnp.arange(owned_len, dtype=jnp.int32)
    pair_at = flat_index // (AW * AW)
    cell_index = flat_index % (AW * AW)
    pair_energy = table_lookup(pair_list[:, 0], occ_energy) + table_lookup(
        pair_list[:, 1], occ_energy
    )
    owned_pair = table_lookup(pair_at, pair_energy)
    energy_a = table_lookup(cell_index // AW, virt_energy)
    energy_b = table_lookup(cell_index % AW, virt_energy)
    denominator = owned_pair - energy_a - energy_b
    return (owned / denominator).reshape(1, owned_len)


def solution(mesh):
    fine = Mesh(mesh.devices.reshape(2, 4, 16, 2, 4), BLK + ("yh",))
    placed = (
        P(BLK + ("yh",), None, None),
        P(BLK, "yh", None),
        P(BLK, "yh", None),
        P(BLK, None),
        P("yh", None),
        P(),
        P(),
    )
    return jax.shard_map(
        shards, mesh=fine, in_specs=placed, out_specs=P("yh", BLK), check_vma=False
    )
```

```python
import jax
import jax.numpy as jnp
from jax import lax
from jax.experimental import pallas as pl
from jax.experimental.pallas import tpu as pltpu
from jax.sharding import Mesh
from jax.sharding import PartitionSpec as P

AW = 16
BLOCK_VIRTUALS = 32
NV = 704
BLK = ("yl", "x", "z", "core")
PLANE = ("yl", "x", "core")
GROUP = 4
LANES = 128
PAIRS = BLOCK_VIRTUALS**2
TOP = 14.0


def swap_lane_blocks(tiles):
    lane = lax.broadcasted_iota(jnp.int32, tiles[0].shape, 1)
    block = lax.shift_right_logical(lane, 5)
    result = []
    for j in range(GROUP):
        out = None
        for i in range(GROUP):
            shift = (i - j) * BLOCK_VIRTUALS % LANES
            moved = pltpu.roll(tiles[i], shift, 1) if shift else tiles[i]
            out = moved if out is None else jnp.where(block == i, moved, out)
        result.append(out)
    return result


def integrals_kernel(picked_ref, out_ref, left_ref, right_ref, product_ref):
    for source in range(0, 16, GROUP):
        for first in range(0, AW, GROUP):
            lanes = slice(first * BLOCK_VIRTUALS, first * BLOCK_VIRTUALS + LANES)
            tiles = [
                picked_ref[source + i, :, lanes].astype(jnp.float32) for i in range(GROUP)
            ]
            depth = slice(source * BLOCK_VIRTUALS, source * BLOCK_VIRTUALS + LANES)
            for j, tile in enumerate(swap_lane_blocks(tiles)):
                rows = slice((first + j) * BLOCK_VIRTUALS, (first + j + 1) * BLOCK_VIRTUALS)
                tile = tile.astype(jnp.bfloat16)
                left_ref[rows, depth] = tile[:BLOCK_VIRTUALS]
                right_ref[rows, depth] = tile[BLOCK_VIRTUALS:]
    product = lax.dot_general(
        left_ref[...],
        right_ref[...],
        (((1,), (1,)), ((), ())),
        preferred_element_type=jnp.float32,
    )
    largest = jnp.max(jnp.max(jnp.abs(product), axis=0, keepdims=True), axis=1, keepdims=True)
    power = jnp.ceil(jnp.log2(jnp.maximum(largest, 2.0**-100)))
    scale = jnp.exp2(TOP - power)
    product_ref[...] = (product * scale).reshape(product_ref.shape)
    out_ref[:, :, PAIRS:] = jnp.broadcast_to(power, (AW * AW, LANES)).reshape(AW, AW, LANES)
    for c in range(0, BLOCK_VIRTUALS, GROUP):
        for b in range(0, AW, GROUP):
            lanes = slice(b * BLOCK_VIRTUALS, b * BLOCK_VIRTUALS + LANES)
            tiles = [product_ref[:, c + i, lanes] for i in range(GROUP)]
            for j, tile in enumerate(swap_lane_blocks(tiles)):
                lanes_out = slice(c * BLOCK_VIRTUALS, c * BLOCK_VIRTUALS + LANES)
                out_ref[b + j, :, lanes_out] = tile


def block_integrals(picked):
    side = AW * BLOCK_VIRTUALS
    return pl.pallas_call(
        integrals_kernel,
        out_shape=jax.ShapeDtypeStruct((AW, AW, PAIRS + LANES), jnp.float32),
        in_specs=[pl.BlockSpec(memory_space=pltpu.VMEM)],
        out_specs=pl.BlockSpec(memory_space=pltpu.VMEM),
        scratch_shapes=[
            pltpu.VMEM((side, side), jnp.bfloat16),
            pltpu.VMEM((side, side), jnp.bfloat16),
            pltpu.VMEM((AW, BLOCK_VIRTUALS, side), jnp.float32),
        ],
        compiler_params=pltpu.CompilerParams(vmem_limit_bytes=24 * 1024 * 1024),
        cost_estimate=pl.CostEstimate(
            flops=2 * side**3, bytes_accessed=2 * 1024 * 1024, transcendentals=0
        ),
        name="block_integrals",
    )(picked)


def table_lookup(index_list, table):
    slots_here = jnp.arange(table.shape[0], dtype=jnp.int32)
    return jnp.sum(
        jnp.where(index_list[:, None] == slots_here[None, :], table[None, :], 0.0), axis=1
    )


def one_hot_rows(columns, width):
    cols = lax.broadcasted_iota(jnp.int32, (columns.shape[0], width), 1)
    return (columns[:, None] == cols).astype(jnp.bfloat16)


def select_rows(hot, rows):
    return lax.dot_general(
        hot, rows, (((1,), (1,)), ((), ())), preferred_element_type=jnp.float32
    ).astype(jnp.bfloat16)


def shards(
    factor, amplitude_forward, amplitude_reversed, block_map, pair_list, virt_energy, occ_energy
):
    plane_map = lax.all_to_all(
        jnp.broadcast_to(block_map, (16, 2)), PLANE, 0, 0, tiled=True
    )
    line = lax.all_gather(factor, "z", axis=0, tiled=True)
    q_line = line.shape[0]
    wanted = (
        plane_map.reshape(-1, 1) * BLOCK_VIRTUALS + jnp.arange(BLOCK_VIRTUALS, dtype=jnp.int32)
    ).reshape(-1)
    line = line.transpose(1, 0, 2).reshape(AW * q_line, NV)
    picked = select_rows(one_hot_rows(wanted, NV), line)
    picked = picked.reshape(16, 2 * BLOCK_VIRTUALS, AW * q_line)
    picked = lax.all_to_all(picked, PLANE, 0, 0, tiled=True)
    partial_sum = block_integrals(picked).astype(jnp.float16).reshape(4, 4 * AW, -1)
    quarters = lax.all_to_all(partial_sum, "yh", 0, 0, tiled=True)
    quarters = quarters.astype(jnp.float32)
    unscale = jnp.exp2(quarters[:, :1, PAIRS : PAIRS + 1] - TOP)
    coulomb = jnp.sum(quarters[:, :, :PAIRS] * unscale, axis=0)
    mirrored = lax.all_gather(coulomb.astype(jnp.bfloat16), "yh", axis=0, tiled=True)
    weights = mirrored.reshape(AW, AW, -1).transpose(1, 0, 2).reshape(AW * AW, -1)
    direct_term = lax.dot_general(
        amplitude_forward[0], weights, (((1,), (1,)), ((), ())), preferred_element_type=jnp.float32
    )
    swapped = lax.dot_general(
        amplitude_reversed[0], mirrored, (((1,), (1,)), ((), ())), preferred_element_type=jnp.float32
    )
    slot_term = (direct_term + swapped).astype(jnp.bfloat16)
    row = jnp.arange(768, dtype=jnp.int32)
    source = jnp.arange(768, dtype=jnp.int32).reshape(8, 16, 2, 3).transpose(0, 2, 1, 3).reshape(-1)
    hot = one_hot_rows(source, 768)
    ordered = lax.dot_general(
        hot, slot_term, (((1,), (0,)), ((), ())), preferred_element_type=jnp.float32
    ).astype(jnp.bfloat16)
    ordered = lax.all_to_all(ordered.reshape(16, 48, 256), PLANE, 0, 0, tiled=True)
    plane_sum = jnp.sum(ordered.astype(jnp.float32), axis=0).reshape(16, 768)
    owned = jnp.sum(lax.all_to_all(plane_sum, "z", 0, 0, tiled=True), axis=0)

    owned_len = owned.shape[0]
    offset = lax.axis_index(BLK) * owned_len
    flat_index = offset + jnp.arange(owned_len, dtype=jnp.int32)
    pair_at = flat_index // (AW * AW)
    cell_index = flat_index % (AW * AW)
    pair_energy = table_lookup(pair_list[:, 0], occ_energy) + table_lookup(
        pair_list[:, 1], occ_energy
    )
    owned_pair = table_lookup(pair_at, pair_energy)
    energy_a = table_lookup(cell_index // AW, virt_energy)
    energy_b = table_lookup(cell_index % AW, virt_energy)
    denominator = owned_pair - energy_a - energy_b
    return (owned / denominator).reshape(1, owned_len)


def solution(mesh):
    fine = Mesh(mesh.devices.reshape(2, 4, 16, 2, 4), BLK + ("yh",))
    placed = (
        P(BLK + ("yh",), None, None),
        P(BLK, "yh", None),
        P(BLK, "yh", None),
        P(BLK, None),
        P("yh", None),
        P(),
        P(),
    )
    return jax.shard_map(
        shards, mesh=fine, in_specs=placed, out_specs=P("yh", BLK), check_vma=False
    )
```

```python
import jax
import jax.numpy as jnp
from jax import lax
from jax.experimental import pallas as pl
from jax.experimental.pallas import tpu as pltpu
from jax.sharding import Mesh
from jax.sharding import PartitionSpec as P

AW = 16
BLOCK_VIRTUALS = 32
NV = 704
BLK = ("yl", "x", "z", "core")
PLANE = ("yl", "x", "core")
GROUP = 4
LANES = 128
PAIRS = BLOCK_VIRTUALS**2
TOP = 14.0


def swap_lane_blocks(tiles):
    lane = lax.broadcasted_iota(jnp.int32, tiles[0].shape, 1)
    block = lax.shift_right_logical(lane, 5)
    result = []
    for j in range(GROUP):
        out = None
        for i in range(GROUP):
            shift = (i - j) * BLOCK_VIRTUALS % LANES
            moved = pltpu.roll(tiles[i], shift, 1) if shift else tiles[i]
            out = moved if out is None else jnp.where(block == i, moved, out)
        result.append(out)
    return result


def integrals_kernel(picked_ref, out_ref, left_ref, right_ref, product_ref):
    for source in range(0, 16, GROUP):
        for first in range(0, AW, GROUP):
            lanes = slice(first * BLOCK_VIRTUALS, first * BLOCK_VIRTUALS + LANES)
            tiles = [
                picked_ref[source + i, :, lanes].astype(jnp.float32) for i in range(GROUP)
            ]
            depth = slice(source * BLOCK_VIRTUALS, source * BLOCK_VIRTUALS + LANES)
            for j, tile in enumerate(swap_lane_blocks(tiles)):
                rows = slice((first + j) * BLOCK_VIRTUALS, (first + j + 1) * BLOCK_VIRTUALS)
                tile = tile.astype(jnp.bfloat16)
                left_ref[rows, depth] = tile[:BLOCK_VIRTUALS]
                right_ref[rows, depth] = tile[BLOCK_VIRTUALS:]
    product = lax.dot_general(
        left_ref[...],
        right_ref[...],
        (((1,), (1,)), ((), ())),
        preferred_element_type=jnp.float32,
    )
    largest = jnp.max(jnp.max(jnp.abs(product), axis=0, keepdims=True), axis=1, keepdims=True)
    power = jnp.ceil(jnp.log2(jnp.maximum(largest, 2.0**-100)))
    scale = jnp.exp2(TOP - power)
    product_ref[...] = (product * scale).reshape(product_ref.shape)
    out_ref[:, :, PAIRS:] = jnp.broadcast_to(power, (AW * AW, LANES)).reshape(AW, AW, LANES)
    for c in range(0, BLOCK_VIRTUALS, GROUP):
        for b in range(0, AW, GROUP):
            lanes = slice(b * BLOCK_VIRTUALS, b * BLOCK_VIRTUALS + LANES)
            tiles = [product_ref[:, c + i, lanes] for i in range(GROUP)]
            for j, tile in enumerate(swap_lane_blocks(tiles)):
                lanes_out = slice(c * BLOCK_VIRTUALS, c * BLOCK_VIRTUALS + LANES)
                out_ref[b + j, :, lanes_out] = tile


def select_matmul(hot, rows):
    return jnp.dot(hot, rows, preferred_element_type=jnp.float32).astype(jnp.bfloat16)


def residual_kernel(forward_ref, reversed_ref, mirrored_ref, out_ref):
    cells = AW * AW
    row = lax.broadcasted_iota(jnp.int32, (cells, cells), 0)
    col = lax.broadcasted_iota(jnp.int32, (cells, cells), 1)
    other = lax.bitwise_and(row, AW - 1) * AW + lax.shift_right_logical(row, 4)
    weights = select_matmul((col == other).astype(jnp.bfloat16), mirrored_ref[...])
    across = (((1,), (1,)), ((), ()))
    piece = 96
    row = lax.broadcasted_iota(jnp.int32, (piece, piece), 0)
    col = lax.broadcasted_iota(jnp.int32, (piece, piece), 1)
    core = (row >= piece // 2).astype(jnp.int32)
    within = row - core * (piece // 2)
    line = lax.shift_right_logical(within * 171, 9)
    hot = (col == line * 3 + within + core * 3).astype(jnp.bfloat16)
    for start in range(0, 768, piece):
        rows = slice(start, start + piece)
        term = lax.dot_general(
            forward_ref[0, rows], weights, across, preferred_element_type=jnp.float32
        ) + lax.dot_general(
            reversed_ref[0, rows], mirrored_ref[...], across, preferred_element_type=jnp.float32
        )
        ordered = select_matmul(hot, term.astype(jnp.bfloat16))
        at = start // (piece // 2)
        out_ref[at] = ordered[: piece // 2]
        out_ref[at + 1] = ordered[piece // 2 :]


def residual_terms(forward, backward, mirrored):
    return pl.pallas_call(
        residual_kernel,
        out_shape=jax.ShapeDtypeStruct((16, 48, AW * AW), jnp.bfloat16),
        in_specs=[pl.BlockSpec(memory_space=pltpu.VMEM)] * 3,
        out_specs=pl.BlockSpec(memory_space=pltpu.VMEM),
        compiler_params=pltpu.CompilerParams(vmem_limit_bytes=24 * 1024 * 1024),
        cost_estimate=pl.CostEstimate(
            flops=4 * 768 * 256 * 1024, bytes_accessed=4 * 1024 * 1024, transcendentals=0
        ),
        name="residual_terms",
    )(forward, backward, mirrored)


def block_integrals(picked):
    side = AW * BLOCK_VIRTUALS
    return pl.pallas_call(
        integrals_kernel,
        out_shape=jax.ShapeDtypeStruct((AW, AW, PAIRS + LANES), jnp.float32),
        in_specs=[pl.BlockSpec(memory_space=pltpu.VMEM)],
        out_specs=pl.BlockSpec(memory_space=pltpu.VMEM),
        scratch_shapes=[
            pltpu.VMEM((side, side), jnp.bfloat16),
            pltpu.VMEM((side, side), jnp.bfloat16),
            pltpu.VMEM((AW, BLOCK_VIRTUALS, side), jnp.float32),
        ],
        compiler_params=pltpu.CompilerParams(vmem_limit_bytes=24 * 1024 * 1024),
        cost_estimate=pl.CostEstimate(
            flops=2 * side**3, bytes_accessed=2 * 1024 * 1024, transcendentals=0
        ),
        name="block_integrals",
    )(picked)


def table_lookup(index_list, table):
    slots_here = jnp.arange(table.shape[0], dtype=jnp.int32)
    return jnp.sum(
        jnp.where(index_list[:, None] == slots_here[None, :], table[None, :], 0.0), axis=1
    )


def one_hot_rows(columns, width):
    cols = lax.broadcasted_iota(jnp.int32, (columns.shape[0], width), 1)
    return (columns[:, None] == cols).astype(jnp.bfloat16)


def select_rows(hot, rows):
    return lax.dot_general(
        hot, rows, (((1,), (1,)), ((), ())), preferred_element_type=jnp.float32
    ).astype(jnp.bfloat16)


def shards(
    factor, amplitude_forward, amplitude_reversed, block_map, pair_list, virt_energy, occ_energy
):
    plane_map = lax.all_to_all(
        jnp.broadcast_to(block_map, (16, 2)), PLANE, 0, 0, tiled=True
    )
    line = lax.all_gather(factor, "z", axis=0, tiled=True)
    q_line = line.shape[0]
    wanted = (
        plane_map.reshape(-1, 1) * BLOCK_VIRTUALS + jnp.arange(BLOCK_VIRTUALS, dtype=jnp.int32)
    ).reshape(-1)
    line = line.transpose(1, 0, 2).reshape(AW * q_line, NV)
    picked = select_rows(one_hot_rows(wanted, NV), line)
    picked = picked.reshape(16, 2 * BLOCK_VIRTUALS, AW * q_line)
    picked = lax.all_to_all(picked, PLANE, 0, 0, tiled=True)
    partial_sum = block_integrals(picked).astype(jnp.float16).reshape(4, 4 * AW, -1)
    quarters = lax.all_to_all(partial_sum, "yh", 0, 0, tiled=True)
    quarters = quarters.astype(jnp.float32)
    unscale = jnp.exp2(quarters[:, :1, PAIRS : PAIRS + 1] - TOP)
    coulomb = jnp.sum(quarters[:, :, :PAIRS] * unscale, axis=0)
    mirrored = lax.all_gather(coulomb.astype(jnp.bfloat16), "yh", axis=0, tiled=True)
    ordered = residual_terms(amplitude_forward, amplitude_reversed, mirrored)
    ordered = lax.all_to_all(ordered, PLANE, 0, 0, tiled=True)
    plane_sum = jnp.sum(ordered.astype(jnp.float32), axis=0).reshape(16, 1, 768)
    owned = jnp.sum(lax.all_to_all(plane_sum, "z", 0, 0, tiled=True), axis=0)

    owned_len = owned.shape[1]
    offset = lax.axis_index(BLK) * owned_len
    flat_index = offset + jnp.arange(owned_len, dtype=jnp.int32)
    pair_at = flat_index // (AW * AW)
    cell_index = flat_index % (AW * AW)
    pair_energy = table_lookup(pair_list[:, 0], occ_energy) + table_lookup(
        pair_list[:, 1], occ_energy
    )
    owned_pair = table_lookup(pair_at, pair_energy)
    energy_a = table_lookup(cell_index // AW, virt_energy)
    energy_b = table_lookup(cell_index % AW, virt_energy)
    denominator = owned_pair - energy_a - energy_b
    return owned / denominator.reshape(1, owned_len)


def solution(mesh):
    fine = Mesh(mesh.devices.reshape(2, 4, 16, 2, 4), BLK + ("yh",))
    placed = (
        P(BLK + ("yh",), None, None),
        P(BLK, "yh", None),
        P(BLK, "yh", None),
        P(BLK, None),
        P("yh", None),
        P(),
        P(),
    )
    return jax.shard_map(
        shards, mesh=fine, in_specs=placed, out_specs=P("yh", BLK), check_vma=False
    )
```

```python
import jax
import jax.numpy as jnp
from jax import lax
from jax.experimental import pallas as pl
from jax.experimental.pallas import tpu as pltpu
from jax.sharding import Mesh
from jax.sharding import PartitionSpec as P

AW = 16
BLOCK_VIRTUALS = 32
NV = 704
BLK = ("yl", "x", "z", "core")
PLANE = ("yl", "x", "core")
GROUP = 4
LANES = 128
PAIRS = BLOCK_VIRTUALS**2
TOP = 14.0


def swap_lane_blocks(tiles):
    lane = lax.broadcasted_iota(jnp.int32, tiles[0].shape, 1)
    block = lax.shift_right_logical(lane, 5)
    result = []
    for j in range(GROUP):
        out = None
        for i in range(GROUP):
            shift = (i - j) * BLOCK_VIRTUALS % LANES
            moved = pltpu.roll(tiles[i], shift, 1) if shift else tiles[i]
            out = moved if out is None else jnp.where(block == i, moved, out)
        result.append(out)
    return result


def integrals_kernel(picked_ref, out_ref, left_ref, right_ref, product_ref):
    for source in range(0, 16, GROUP):
        for first in range(0, AW, GROUP):
            lanes = slice(first * BLOCK_VIRTUALS, first * BLOCK_VIRTUALS + LANES)
            tiles = [
                picked_ref[source + i, :, lanes].astype(jnp.float32) for i in range(GROUP)
            ]
            depth = slice(source * BLOCK_VIRTUALS, source * BLOCK_VIRTUALS + LANES)
            for j, tile in enumerate(swap_lane_blocks(tiles)):
                rows = slice((first + j) * BLOCK_VIRTUALS, (first + j + 1) * BLOCK_VIRTUALS)
                tile = tile.astype(jnp.bfloat16)
                left_ref[rows, depth] = tile[:BLOCK_VIRTUALS]
                right_ref[rows, depth] = tile[BLOCK_VIRTUALS:]
    product = lax.dot_general(
        left_ref[...],
        right_ref[...],
        (((1,), (1,)), ((), ())),
        preferred_element_type=jnp.float32,
    )
    largest = jnp.max(jnp.max(jnp.abs(product), axis=0, keepdims=True), axis=1, keepdims=True)
    power = jnp.ceil(jnp.log2(jnp.maximum(largest, 2.0**-100)))
    scale = jnp.exp2(TOP - power)
    product_ref[...] = (product * scale).reshape(product_ref.shape)
    out_ref[:, :, PAIRS:] = jnp.broadcast_to(power, (AW * AW, LANES)).reshape(AW, AW, LANES)
    for c in range(0, BLOCK_VIRTUALS, GROUP):
        for b in range(0, AW, GROUP):
            lanes = slice(b * BLOCK_VIRTUALS, b * BLOCK_VIRTUALS + LANES)
            tiles = [product_ref[:, c + i, lanes] for i in range(GROUP)]
            for j, tile in enumerate(swap_lane_blocks(tiles)):
                lanes_out = slice(c * BLOCK_VIRTUALS, c * BLOCK_VIRTUALS + LANES)
                out_ref[b + j, :, lanes_out] = tile


def select_matmul(hot, rows):
    return jnp.dot(hot, rows, preferred_element_type=jnp.float32).astype(jnp.bfloat16)


def residual_kernel(forward_ref, reversed_ref, mirrored_ref, out_ref, term_ref):
    cells = AW * AW
    row = lax.broadcasted_iota(jnp.int32, (cells, cells), 0)
    col = lax.broadcasted_iota(jnp.int32, (cells, cells), 1)
    other = lax.bitwise_and(row, AW - 1) * AW + lax.shift_right_logical(row, 4)
    hot = (col == other).astype(jnp.bfloat16)
    weights = select_matmul(hot, mirrored_ref[...])
    across = (((1,), (1,)), ((), ()))
    term_ref[...] = (
        lax.dot_general(
            forward_ref[0], weights, across, preferred_element_type=jnp.float32
        )
        + lax.dot_general(
            reversed_ref[0], mirrored_ref[...], across, preferred_element_type=jnp.float32
        )
    ).astype(jnp.bfloat16)
    piece = 96
    row = lax.broadcasted_iota(jnp.int32, (piece, piece), 0)
    col = lax.broadcasted_iota(jnp.int32, (piece, piece), 1)
    core = (row >= piece // 2).astype(jnp.int32)
    within = row - core * (piece // 2)
    line = lax.shift_right_logical(within * 171, 9)
    hot = (col == line * 3 + within + core * 3).astype(jnp.bfloat16)
    for at in range(8):
        ordered = select_matmul(hot, term_ref[at * piece : (at + 1) * piece])
        rows = slice(at // 4 * (piece // 2), (at // 4 + 1) * (piece // 2))
        out_ref[at % 4 * 2, rows] = ordered[: piece // 2]
        out_ref[at % 4 * 2 + 1, rows] = ordered[piece // 2 :]


def residual_terms(forward, backward, mirrored):
    return pl.pallas_call(
        residual_kernel,
        out_shape=jax.ShapeDtypeStruct((8, 96, AW * AW), jnp.bfloat16),
        in_specs=[pl.BlockSpec(memory_space=pltpu.VMEM)] * 3,
        out_specs=pl.BlockSpec(memory_space=pltpu.VMEM),
        scratch_shapes=[pltpu.VMEM((768, AW * AW), jnp.bfloat16)],
        compiler_params=pltpu.CompilerParams(vmem_limit_bytes=24 * 1024 * 1024),
        cost_estimate=pl.CostEstimate(
            flops=4 * 768 * 256 * 1024, bytes_accessed=4 * 1024 * 1024, transcendentals=0
        ),
        name="residual_terms",
    )(forward, backward, mirrored)


def block_integrals(picked):
    side = AW * BLOCK_VIRTUALS
    return pl.pallas_call(
        integrals_kernel,
        out_shape=jax.ShapeDtypeStruct((AW, AW, PAIRS + LANES), jnp.float32),
        in_specs=[pl.BlockSpec(memory_space=pltpu.VMEM)],
        out_specs=pl.BlockSpec(memory_space=pltpu.VMEM),
        scratch_shapes=[
            pltpu.VMEM((side, side), jnp.bfloat16),
            pltpu.VMEM((side, side), jnp.bfloat16),
            pltpu.VMEM((AW, BLOCK_VIRTUALS, side), jnp.float32),
        ],
        compiler_params=pltpu.CompilerParams(vmem_limit_bytes=24 * 1024 * 1024),
        cost_estimate=pl.CostEstimate(
            flops=2 * side**3, bytes_accessed=2 * 1024 * 1024, transcendentals=0
        ),
        name="block_integrals",
    )(picked)


def table_lookup(index_list, table):
    slots_here = jnp.arange(table.shape[0], dtype=jnp.int32)
    return jnp.sum(
        jnp.where(index_list[:, None] == slots_here[None, :], table[None, :], 0.0), axis=1
    )


def one_hot_rows(columns, width):
    cols = lax.broadcasted_iota(jnp.int32, (columns.shape[0], width), 1)
    return (columns[:, None] == cols).astype(jnp.bfloat16)


def select_rows(hot, rows):
    return lax.dot_general(
        hot, rows, (((1,), (1,)), ((), ())), preferred_element_type=jnp.float32
    ).astype(jnp.bfloat16)


def shards(
    factor, amplitude_forward, amplitude_reversed, block_map, pair_list, virt_energy, occ_energy
):
    plane_map = lax.all_to_all(
        jnp.broadcast_to(block_map, (16, 2)), PLANE, 0, 0, tiled=True
    )
    line = lax.all_gather(factor, "z", axis=0, tiled=True)
    q_line = line.shape[0]
    wanted = (
        plane_map.reshape(-1, 1) * BLOCK_VIRTUALS + jnp.arange(BLOCK_VIRTUALS, dtype=jnp.int32)
    ).reshape(-1)
    line = line.transpose(1, 0, 2).reshape(AW * q_line, NV)
    picked = select_rows(one_hot_rows(wanted, NV), line)
    picked = picked.reshape(16, 2 * BLOCK_VIRTUALS, AW * q_line)
    picked = lax.all_to_all(picked, PLANE, 0, 0, tiled=True)
    partial_sum = block_integrals(picked).astype(jnp.float16).reshape(4, 4 * AW, -1)
    quarters = lax.all_to_all(partial_sum, "yh", 0, 0, tiled=True)
    quarters = quarters.astype(jnp.float32)
    unscale = jnp.exp2(quarters[:, :1, PAIRS : PAIRS + 1] - TOP)
    coulomb = jnp.sum(quarters[:, :, :PAIRS] * unscale, axis=0)
    mirrored = lax.all_gather(coulomb.astype(jnp.bfloat16), "yh", axis=0, tiled=True)
    ordered = residual_terms(amplitude_forward, amplitude_reversed, mirrored)
    ordered = lax.all_to_all(ordered, ("x", "core"), 0, 0, tiled=True)
    near_sum = jnp.sum(ordered.astype(jnp.float32), axis=0).reshape(32, 1, 768)
    owned = jnp.sum(lax.all_to_all(near_sum, ("yl", "z"), 0, 0, tiled=True), axis=0)

    owned_len = owned.shape[1]
    offset = lax.axis_index(BLK) * owned_len
    flat_index = offset + jnp.arange(owned_len, dtype=jnp.int32)
    pair_at = flat_index // (AW * AW)
    cell_index = flat_index % (AW * AW)
    pair_energy = table_lookup(pair_list[:, 0], occ_energy) + table_lookup(
        pair_list[:, 1], occ_energy
    )
    owned_pair = table_lookup(pair_at, pair_energy)
    energy_a = table_lookup(cell_index // AW, virt_energy)
    energy_b = table_lookup(cell_index % AW, virt_energy)
    denominator = owned_pair - energy_a - energy_b
    return owned / denominator.reshape(1, owned_len)


def solution(mesh):
    fine = Mesh(mesh.devices.reshape(2, 4, 16, 2, 4), BLK + ("yh",))
    placed = (
        P(BLK + ("yh",), None, None),
        P(BLK, "yh", None),
        P(BLK, "yh", None),
        P(BLK, None),
        P("yh", None),
        P(),
        P(),
    )
    return jax.shard_map(
        shards, mesh=fine, in_specs=placed, out_specs=P("yh", BLK), check_vma=False
    )
```

```python
import jax
import jax.numpy as jnp
from jax import lax
from jax.experimental import pallas as pl
from jax.experimental.pallas import tpu as pltpu
from jax.sharding import Mesh
from jax.sharding import PartitionSpec as P

AW = 16
BLOCK_VIRTUALS = 32
NV = 704
BLK = ("yl", "x", "z", "core")
PLANE = ("yl", "x", "core")
GROUP = 4
LANES = 128
PAIRS = BLOCK_VIRTUALS**2
TOP = 14.0


def swap_lane_blocks(tiles):
    lane = lax.broadcasted_iota(jnp.int32, tiles[0].shape, 1)
    block = lax.shift_right_logical(lane, 5)
    result = []
    for j in range(GROUP):
        out = None
        for i in range(GROUP):
            shift = (i - j) * BLOCK_VIRTUALS % LANES
            moved = pltpu.roll(tiles[i], shift, 1) if shift else tiles[i]
            out = moved if out is None else jnp.where(block == i, moved, out)
        result.append(out)
    return result


def integrals_kernel(picked_ref, out_ref, left_ref, right_ref, product_ref):
    for source in range(0, 16, GROUP):
        for first in range(0, AW, GROUP):
            lanes = slice(first * BLOCK_VIRTUALS, first * BLOCK_VIRTUALS + LANES)
            tiles = [
                picked_ref[source + i, :, lanes].astype(jnp.float32) for i in range(GROUP)
            ]
            depth = slice(source * BLOCK_VIRTUALS, source * BLOCK_VIRTUALS + LANES)
            for j, tile in enumerate(swap_lane_blocks(tiles)):
                rows = slice((first + j) * BLOCK_VIRTUALS, (first + j + 1) * BLOCK_VIRTUALS)
                tile = tile.astype(jnp.bfloat16)
                left_ref[rows, depth] = tile[:BLOCK_VIRTUALS]
                right_ref[rows, depth] = tile[BLOCK_VIRTUALS:]
    product = lax.dot_general(
        left_ref[...],
        right_ref[...],
        (((1,), (1,)), ((), ())),
        preferred_element_type=jnp.float32,
    )
    largest = jnp.max(jnp.max(jnp.abs(product), axis=0, keepdims=True), axis=1, keepdims=True)
    power = jnp.ceil(jnp.log2(jnp.maximum(largest, 2.0**-100)))
    scale = jnp.exp2(TOP - power)
    product_ref[...] = (product * scale).reshape(product_ref.shape)
    out_ref[:, :, PAIRS:] = jnp.broadcast_to(power, (AW * AW, LANES)).reshape(AW, AW, LANES)
    for c in range(0, BLOCK_VIRTUALS, GROUP):
        for b in range(0, AW, GROUP):
            lanes = slice(b * BLOCK_VIRTUALS, b * BLOCK_VIRTUALS + LANES)
            tiles = [product_ref[:, c + i, lanes] for i in range(GROUP)]
            for j, tile in enumerate(swap_lane_blocks(tiles)):
                lanes_out = slice(c * BLOCK_VIRTUALS, c * BLOCK_VIRTUALS + LANES)
                out_ref[b + j, :, lanes_out] = tile


def select_matmul(hot, rows):
    return jnp.dot(hot, rows, preferred_element_type=jnp.float32).astype(jnp.bfloat16)


def residual_kernel(forward_ref, reversed_ref, mirrored_ref, out_ref, term_ref):
    cells = AW * AW
    row = lax.broadcasted_iota(jnp.int32, (cells, cells), 0)
    col = lax.broadcasted_iota(jnp.int32, (cells, cells), 1)
    other = lax.bitwise_and(row, AW - 1) * AW + lax.shift_right_logical(row, 4)
    hot = (col == other).astype(jnp.bfloat16)
    weights = select_matmul(hot, mirrored_ref[...])
    across = (((1,), (1,)), ((), ()))
    term_ref[...] = (
        lax.dot_general(
            forward_ref[0], weights, across, preferred_element_type=jnp.float32
        )
        + lax.dot_general(
            reversed_ref[0], mirrored_ref[...], across, preferred_element_type=jnp.float32
        )
    ).astype(jnp.bfloat16)
    piece = 96
    row = lax.broadcasted_iota(jnp.int32, (piece, piece), 0)
    col = lax.broadcasted_iota(jnp.int32, (piece, piece), 1)
    core = (row >= piece // 2).astype(jnp.int32)
    within = row - core * (piece // 2)
    line = lax.shift_right_logical(within * 171, 9)
    hot = (col == line * 3 + within + core * 3).astype(jnp.bfloat16)
    for at in range(8):
        ordered = select_matmul(hot, term_ref[at * piece : (at + 1) * piece])
        out_ref[at * 2] = ordered[: piece // 2]
        out_ref[at * 2 + 1] = ordered[piece // 2 :]


def residual_terms(forward, backward, mirrored):
    return pl.pallas_call(
        residual_kernel,
        out_shape=jax.ShapeDtypeStruct((16, 48, AW * AW), jnp.bfloat16),
        in_specs=[pl.BlockSpec(memory_space=pltpu.VMEM)] * 3,
        out_specs=pl.BlockSpec(memory_space=pltpu.VMEM),
        scratch_shapes=[pltpu.VMEM((768, AW * AW), jnp.bfloat16)],
        compiler_params=pltpu.CompilerParams(vmem_limit_bytes=24 * 1024 * 1024),
        cost_estimate=pl.CostEstimate(
            flops=4 * 768 * 256 * 1024, bytes_accessed=4 * 1024 * 1024, transcendentals=0
        ),
        name="residual_terms",
    )(forward, backward, mirrored)


def block_integrals(picked):
    side = AW * BLOCK_VIRTUALS
    return pl.pallas_call(
        integrals_kernel,
        out_shape=jax.ShapeDtypeStruct((AW, AW, PAIRS + LANES), jnp.float32),
        in_specs=[pl.BlockSpec(memory_space=pltpu.VMEM)],
        out_specs=pl.BlockSpec(memory_space=pltpu.VMEM),
        scratch_shapes=[
            pltpu.VMEM((side, side), jnp.bfloat16),
            pltpu.VMEM((side, side), jnp.bfloat16),
            pltpu.VMEM((AW, BLOCK_VIRTUALS, side), jnp.float32),
        ],
        compiler_params=pltpu.CompilerParams(vmem_limit_bytes=24 * 1024 * 1024),
        cost_estimate=pl.CostEstimate(
            flops=2 * side**3, bytes_accessed=2 * 1024 * 1024, transcendentals=0
        ),
        name="block_integrals",
    )(picked)


def table_lookup(index_list, table):
    slots_here = jnp.arange(table.shape[0], dtype=jnp.int32)
    return jnp.sum(
        jnp.where(index_list[:, None] == slots_here[None, :], table[None, :], 0.0), axis=1
    )


def one_hot_rows(columns, width):
    cols = lax.broadcasted_iota(jnp.int32, (columns.shape[0], width), 1)
    return (columns[:, None] == cols).astype(jnp.bfloat16)


def select_rows(hot, rows):
    return lax.dot_general(
        hot, rows, (((1,), (1,)), ((), ())), preferred_element_type=jnp.float32
    ).astype(jnp.bfloat16)


def shards(
    factor, amplitude_forward, amplitude_reversed, block_map, pair_list, virt_energy, occ_energy
):
    plane_map = lax.all_to_all(
        jnp.broadcast_to(block_map, (16, 2)), PLANE, 0, 0, tiled=True
    )
    line = lax.all_gather(factor, "z", axis=0, tiled=True)
    q_line = line.shape[0]
    wanted = (
        plane_map.reshape(-1, 1) * BLOCK_VIRTUALS + jnp.arange(BLOCK_VIRTUALS, dtype=jnp.int32)
    ).reshape(-1)
    line = line.transpose(1, 0, 2).reshape(AW * q_line, NV)
    picked = select_rows(one_hot_rows(wanted, NV), line)
    picked = picked.reshape(16, 2 * BLOCK_VIRTUALS, AW * q_line)
    picked = lax.all_to_all(picked, PLANE, 0, 0, tiled=True)
    partial_sum = block_integrals(picked).astype(jnp.float16).reshape(4, 4 * AW, -1)
    quarters = lax.all_to_all(partial_sum, "yh", 0, 0, tiled=True)
    quarters = quarters.astype(jnp.float32)
    unscale = jnp.exp2(quarters[:, :1, PAIRS : PAIRS + 1] - TOP)
    coulomb = jnp.sum(quarters[:, :, :PAIRS] * unscale, axis=0)
    mirrored = lax.all_gather(coulomb.astype(jnp.bfloat16), "yh", axis=0, tiled=True)
    ordered = residual_terms(amplitude_forward, amplitude_reversed, mirrored)
    ordered = lax.all_to_all(ordered, PLANE, 0, 0, tiled=True)
    plane_sum = jnp.sum(ordered.astype(jnp.float32), axis=0).reshape(16, 1, 768)
    owned = jnp.sum(lax.all_to_all(plane_sum, "z", 0, 0, tiled=True), axis=0)

    owned_len = owned.shape[1]
    offset = lax.axis_index(BLK) * owned_len
    flat_index = offset + jnp.arange(owned_len, dtype=jnp.int32)
    pair_at = flat_index // (AW * AW)
    cell_index = flat_index % (AW * AW)
    pair_energy = table_lookup(pair_list[:, 0], occ_energy) + table_lookup(
        pair_list[:, 1], occ_energy
    )
    owned_pair = table_lookup(pair_at, pair_energy)
    energy_a = table_lookup(cell_index // AW, virt_energy)
    energy_b = table_lookup(cell_index % AW, virt_energy)
    denominator = owned_pair - energy_a - energy_b
    return owned / denominator.reshape(1, owned_len)


def solution(mesh):
    fine = Mesh(mesh.devices.reshape(2, 4, 16, 2, 4), BLK + ("yh",))
    placed = (
        P(BLK + ("yh",), None, None),
        P(BLK, "yh", None),
        P(BLK, "yh", None),
        P(BLK, None),
        P("yh", None),
        P(),
        P(),
    )
    return jax.shard_map(
        shards, mesh=fine, in_specs=placed, out_specs=P("yh", BLK), check_vma=False
    )
```

```python
import jax
import jax.numpy as jnp
from jax import lax
from jax.experimental import pallas as pl
from jax.experimental.pallas import tpu as pltpu
from jax.sharding import Mesh
from jax.sharding import PartitionSpec as P

AW = 16
BLOCK_VIRTUALS = 32
NV = 704
BLK = ("yl", "x", "z8", "zp", "core")
NEAR = ("yl", "x", "zp", "core")
PLANE = ("yl", "x", "core")
GROUP = 4
LANES = 128
PAIRS = BLOCK_VIRTUALS**2
TOP = 14.0


def swap_lane_blocks(tiles, width):
    tiles = list(tiles)
    lane = lax.broadcasted_iota(jnp.int32, tiles[0].shape, 1)
    step = 1
    while step < len(tiles):
        low = lax.bitwise_and(lane, step * width) == 0
        for i in range(len(tiles)):
            if i & step == 0:
                first, second = tiles[i], tiles[i + step]
                tiles[i] = jnp.where(low, first, pltpu.roll(second, step * width, 1))
                tiles[i + step] = jnp.where(
                    low, pltpu.roll(first, LANES - step * width, 1), second
                )
        step *= 2
    return tiles


def integrals_kernel(picked_ref, out_ref, left_ref, right_ref, product_ref):
    q_line = picked_ref.shape[2] // AW
    count = LANES // q_line
    for source in range(0, picked_ref.shape[0], count):
        for first in range(0, AW, count):
            lanes = slice(first * q_line, first * q_line + LANES)
            tiles = [picked_ref[source + i, :, lanes].astype(jnp.float32) for i in range(count)]
            depth = slice(source * q_line, source * q_line + LANES)
            for j, tile in enumerate(swap_lane_blocks(tiles, q_line)):
                rows = slice((first + j) * BLOCK_VIRTUALS, (first + j + 1) * BLOCK_VIRTUALS)
                tile = tile.astype(jnp.bfloat16)
                left_ref[rows, depth] = tile[:BLOCK_VIRTUALS]
                right_ref[rows, depth] = tile[BLOCK_VIRTUALS:]
    product = lax.dot_general(
        left_ref[...],
        right_ref[...],
        (((1,), (1,)), ((), ())),
        preferred_element_type=jnp.float32,
    )
    largest = jnp.max(jnp.max(jnp.abs(product), axis=0, keepdims=True), axis=1, keepdims=True)
    power = jnp.ceil(jnp.log2(jnp.maximum(largest, 2.0**-100)))
    scale = jnp.exp2(TOP - power)
    product_ref[...] = (product * scale).reshape(product_ref.shape)
    out_ref[:, :, PAIRS:] = jnp.broadcast_to(power, (AW * AW, LANES)).reshape(AW, AW, LANES)
    for c in range(0, BLOCK_VIRTUALS, GROUP):
        for b in range(0, AW, GROUP):
            lanes = slice(b * BLOCK_VIRTUALS, b * BLOCK_VIRTUALS + LANES)
            tiles = [product_ref[:, c + i, lanes] for i in range(GROUP)]
            for j, tile in enumerate(swap_lane_blocks(tiles, BLOCK_VIRTUALS)):
                lanes_out = slice(c * BLOCK_VIRTUALS, c * BLOCK_VIRTUALS + LANES)
                out_ref[b + j, :, lanes_out] = tile


def select_matmul(hot, rows):
    return jnp.dot(hot, rows, preferred_element_type=jnp.float32).astype(jnp.bfloat16)


def residual_kernel(forward_ref, reversed_ref, mirrored_ref, out_ref, term_ref):
    cells = AW * AW
    row = lax.broadcasted_iota(jnp.int32, (cells, cells), 0)
    col = lax.broadcasted_iota(jnp.int32, (cells, cells), 1)
    other = lax.bitwise_and(row, AW - 1) * AW + lax.shift_right_logical(row, 4)
    hot = (col == other).astype(jnp.bfloat16)
    weights = select_matmul(hot, mirrored_ref[...])
    across = (((1,), (1,)), ((), ()))
    term_ref[...] = (
        lax.dot_general(
            forward_ref[0], weights, across, preferred_element_type=jnp.float32
        )
        + lax.dot_general(
            reversed_ref[0], mirrored_ref[...], across, preferred_element_type=jnp.float32
        )
    ).astype(jnp.bfloat16)
    piece = 96
    row = lax.broadcasted_iota(jnp.int32, (piece, piece), 0)
    col = lax.broadcasted_iota(jnp.int32, (piece, piece), 1)
    core = (row >= piece // 2).astype(jnp.int32)
    within = row - core * (piece // 2)
    line = lax.shift_right_logical(within * 171, 9)
    hot = (col == line * 3 + within + core * 3).astype(jnp.bfloat16)
    for at in range(8):
        ordered = select_matmul(hot, term_ref[at * piece : (at + 1) * piece])
        out_ref[at * 2] = ordered[: piece // 2]
        out_ref[at * 2 + 1] = ordered[piece // 2 :]


def residual_terms(forward, backward, mirrored):
    return pl.pallas_call(
        residual_kernel,
        out_shape=jax.ShapeDtypeStruct((16, 48, AW * AW), jnp.bfloat16),
        in_specs=[pl.BlockSpec(memory_space=pltpu.VMEM)] * 3,
        out_specs=pl.BlockSpec(memory_space=pltpu.VMEM),
        scratch_shapes=[pltpu.VMEM((768, AW * AW), jnp.bfloat16)],
        compiler_params=pltpu.CompilerParams(vmem_limit_bytes=24 * 1024 * 1024),
        cost_estimate=pl.CostEstimate(
            flops=4 * 768 * 256 * 1024, bytes_accessed=4 * 1024 * 1024, transcendentals=0
        ),
        name="residual_terms",
    )(forward, backward, mirrored)


def block_integrals(picked):
    side = AW * BLOCK_VIRTUALS
    return pl.pallas_call(
        integrals_kernel,
        out_shape=jax.ShapeDtypeStruct((AW, AW, PAIRS + LANES), jnp.float32),
        in_specs=[pl.BlockSpec(memory_space=pltpu.VMEM)],
        out_specs=pl.BlockSpec(memory_space=pltpu.VMEM),
        scratch_shapes=[
            pltpu.VMEM((side, side), jnp.bfloat16),
            pltpu.VMEM((side, side), jnp.bfloat16),
            pltpu.VMEM((AW, BLOCK_VIRTUALS, side), jnp.float32),
        ],
        compiler_params=pltpu.CompilerParams(vmem_limit_bytes=24 * 1024 * 1024),
        cost_estimate=pl.CostEstimate(
            flops=2 * side**3, bytes_accessed=2 * 1024 * 1024, transcendentals=0
        ),
        name="block_integrals",
    )(picked)


def table_lookup(index_list, table):
    slots_here = jnp.arange(table.shape[0], dtype=jnp.int32)
    return jnp.sum(
        jnp.where(index_list[:, None] == slots_here[None, :], table[None, :], 0.0), axis=1
    )


def one_hot_rows(columns, width):
    cols = lax.broadcasted_iota(jnp.int32, (columns.shape[0], width), 1)
    return (columns[:, None] == cols).astype(jnp.bfloat16)


def select_rows(hot, rows):
    return lax.dot_general(
        hot, rows, (((1,), (1,)), ((), ())), preferred_element_type=jnp.float32
    ).astype(jnp.bfloat16)


def shards(
    factor, amplitude_forward, amplitude_reversed, block_map, pair_list, virt_energy, occ_energy
):
    plane_map = lax.all_to_all(
        jnp.broadcast_to(block_map, (32, 2)), NEAR, 0, 0, tiled=True
    )
    line = lax.all_gather(factor, "z8", axis=0, tiled=True)
    q_line = line.shape[0]
    wanted = (
        plane_map.reshape(-1, 1) * BLOCK_VIRTUALS + jnp.arange(BLOCK_VIRTUALS, dtype=jnp.int32)
    ).reshape(-1)
    line = line.transpose(1, 0, 2).reshape(AW * q_line, NV)
    picked = select_rows(one_hot_rows(wanted, NV), line)
    picked = picked.reshape(32, 2 * BLOCK_VIRTUALS, AW * q_line)
    picked = lax.all_to_all(picked, NEAR, 0, 0, tiled=True)
    partial_sum = block_integrals(picked).astype(jnp.float16).reshape(4, 4 * AW, -1)
    quarters = lax.all_to_all(partial_sum, "yh", 0, 0, tiled=True)
    quarters = quarters.astype(jnp.float32)
    unscale = jnp.exp2(quarters[:, :1, PAIRS : PAIRS + 1] - TOP)
    coulomb = jnp.sum(quarters[:, :, :PAIRS] * unscale, axis=0)
    mirrored = lax.all_gather(coulomb.astype(jnp.bfloat16), "yh", axis=0, tiled=True)
    ordered = residual_terms(amplitude_forward, amplitude_reversed, mirrored)
    ordered = lax.all_to_all(ordered, PLANE, 0, 0, tiled=True)
    plane_sum = jnp.sum(ordered.astype(jnp.float32), axis=0).reshape(16, 1, 768)
    owned = jnp.sum(lax.all_to_all(plane_sum, ("z8", "zp"), 0, 0, tiled=True), axis=0)

    owned_len = owned.shape[1]
    offset = lax.axis_index(BLK) * owned_len
    flat_index = offset + jnp.arange(owned_len, dtype=jnp.int32)
    pair_at = flat_index // (AW * AW)
    cell_index = flat_index % (AW * AW)
    pair_energy = table_lookup(pair_list[:, 0], occ_energy) + table_lookup(
        pair_list[:, 1], occ_energy
    )
    owned_pair = table_lookup(pair_at, pair_energy)
    energy_a = table_lookup(cell_index // AW, virt_energy)
    energy_b = table_lookup(cell_index % AW, virt_energy)
    denominator = owned_pair - energy_a - energy_b
    return owned / denominator.reshape(1, owned_len)


def solution(mesh):
    fine = Mesh(mesh.devices.reshape(2, 4, 8, 2, 2, 4), BLK + ("yh",))
    placed = (
        P(BLK + ("yh",), None, None),
        P(BLK, "yh", None),
        P(BLK, "yh", None),
        P(BLK, None),
        P("yh", None),
        P(),
        P(),
    )
    return jax.shard_map(
        shards, mesh=fine, in_specs=placed, out_specs=P("yh", BLK), check_vma=False
    )
```

```python
import jax
import jax.numpy as jnp
from jax import lax
from jax.experimental import pallas as pl
from jax.experimental.pallas import tpu as pltpu
from jax.sharding import Mesh
from jax.sharding import PartitionSpec as P

AW = 16
BLOCK_VIRTUALS = 32
NV = 704
BLK = ("yl", "x", "z", "core")
PLANE = ("yl", "x", "core")
GROUP = 4
LANES = 128
PAIRS = BLOCK_VIRTUALS**2
TOP = 14.0
QUARTER = GROUP * PAIRS


def swap_lane_blocks(tiles):
    lane = lax.broadcasted_iota(jnp.int32, tiles[0].shape, 1)
    block = lax.shift_right_logical(lane, 5)
    result = []
    for j in range(GROUP):
        out = None
        for i in range(GROUP):
            shift = (i - j) * BLOCK_VIRTUALS % LANES
            moved = pltpu.roll(tiles[i], shift, 1) if shift else tiles[i]
            out = moved if out is None else jnp.where(block == i, moved, out)
        result.append(out)
    return result


def integrals_kernel(picked_ref, out_ref, left_ref, right_ref, product_ref):
    for source in range(0, 16, GROUP):
        for first in range(0, AW, GROUP):
            lanes = slice(first * BLOCK_VIRTUALS, first * BLOCK_VIRTUALS + LANES)
            tiles = [
                picked_ref[source + i, :, lanes].astype(jnp.float32) for i in range(GROUP)
            ]
            depth = slice(source * BLOCK_VIRTUALS, source * BLOCK_VIRTUALS + LANES)
            for j, tile in enumerate(swap_lane_blocks(tiles)):
                rows = slice((first + j) * BLOCK_VIRTUALS, (first + j + 1) * BLOCK_VIRTUALS)
                tile = tile.astype(jnp.bfloat16)
                left_ref[rows, depth] = tile[:BLOCK_VIRTUALS]
                right_ref[rows, depth] = tile[BLOCK_VIRTUALS:]
    product = lax.dot_general(
        left_ref[...],
        right_ref[...],
        (((1,), (1,)), ((), ())),
        preferred_element_type=jnp.float32,
    )
    largest = jnp.max(jnp.max(jnp.abs(product), axis=0, keepdims=True), axis=1, keepdims=True)
    power = jnp.ceil(jnp.log2(jnp.maximum(largest, 2.0**-100)))
    scale = jnp.exp2(TOP - power)
    product_ref[...] = (product * scale).reshape(product_ref.shape)
    out_ref[:, :, QUARTER:] = jnp.broadcast_to(power, (GROUP * AW, LANES)).reshape(GROUP, AW, LANES)
    for c in range(0, BLOCK_VIRTUALS, GROUP):
        for b in range(0, AW, GROUP):
            lanes = slice(b * BLOCK_VIRTUALS, b * BLOCK_VIRTUALS + LANES)
            tiles = [product_ref[:, c + i, lanes] for i in range(GROUP)]
            for j, tile in enumerate(swap_lane_blocks(tiles)):
                at = j * PAIRS + c * BLOCK_VIRTUALS
                out_ref[b // GROUP, :, at : at + LANES] = tile


def select_matmul(hot, rows):
    return jnp.dot(hot, rows, preferred_element_type=jnp.float32).astype(jnp.bfloat16)


def residual_kernel(forward_ref, reversed_ref, gathered_ref, out_ref, term_ref, mirrored_ref):
    for b in range(AW):
        rows = slice(b // GROUP * AW, (b // GROUP + 1) * AW)
        lanes = slice(b % GROUP * PAIRS, (b % GROUP + 1) * PAIRS)
        mirrored_ref[b * AW : (b + 1) * AW] = gathered_ref[rows, lanes]
    cells = AW * AW
    row = lax.broadcasted_iota(jnp.int32, (cells, cells), 0)
    col = lax.broadcasted_iota(jnp.int32, (cells, cells), 1)
    other = lax.bitwise_and(row, AW - 1) * AW + lax.shift_right_logical(row, 4)
    hot = (col == other).astype(jnp.bfloat16)
    weights = select_matmul(hot, mirrored_ref[...])
    across = (((1,), (1,)), ((), ()))
    term_ref[...] = (
        lax.dot_general(
            forward_ref[0], weights, across, preferred_element_type=jnp.float32
        )
        + lax.dot_general(
            reversed_ref[0], mirrored_ref[...], across, preferred_element_type=jnp.float32
        )
    ).astype(jnp.bfloat16)
    piece = 96
    row = lax.broadcasted_iota(jnp.int32, (piece, piece), 0)
    col = lax.broadcasted_iota(jnp.int32, (piece, piece), 1)
    core = (row >= piece // 2).astype(jnp.int32)
    within = row - core * (piece // 2)
    line = lax.shift_right_logical(within * 171, 9)
    hot = (col == line * 3 + within + core * 3).astype(jnp.bfloat16)
    for at in range(8):
        ordered = select_matmul(hot, term_ref[at * piece : (at + 1) * piece])
        out_ref[at * 2] = ordered[: piece // 2]
        out_ref[at * 2 + 1] = ordered[piece // 2 :]


def residual_terms(forward, backward, gathered):
    return pl.pallas_call(
        residual_kernel,
        out_shape=jax.ShapeDtypeStruct((16, 48, AW * AW), jnp.bfloat16),
        in_specs=[pl.BlockSpec(memory_space=pltpu.VMEM)] * 3,
        out_specs=pl.BlockSpec(memory_space=pltpu.VMEM),
        scratch_shapes=[
            pltpu.VMEM((768, AW * AW), jnp.bfloat16),
            pltpu.VMEM((AW * AW, PAIRS), jnp.bfloat16),
        ],
        compiler_params=pltpu.CompilerParams(vmem_limit_bytes=24 * 1024 * 1024),
        cost_estimate=pl.CostEstimate(
            flops=4 * 768 * 256 * 1024, bytes_accessed=4 * 1024 * 1024, transcendentals=0
        ),
        name="residual_terms",
    )(forward, backward, gathered)


def plane_sum_kernel(terms_ref, out_ref, total_ref):
    total = terms_ref[0].astype(jnp.float32)
    for source in range(1, 16):
        total = total + terms_ref[source].astype(jnp.float32)
    total_ref[...] = total
    cells = AW * AW
    for z in range(16):
        for k in range(3):
            out_ref[z, :, k * cells : (k + 1) * cells] = total_ref[z * 3 + k : z * 3 + k + 1]


def plane_sums(terms):
    return pl.pallas_call(
        plane_sum_kernel,
        out_shape=jax.ShapeDtypeStruct((16, 1, 768), jnp.float32),
        in_specs=[pl.BlockSpec(memory_space=pltpu.VMEM)],
        out_specs=pl.BlockSpec(memory_space=pltpu.VMEM),
        scratch_shapes=[pltpu.VMEM((48, AW * AW), jnp.float32)],
        compiler_params=pltpu.CompilerParams(vmem_limit_bytes=8 * 1024 * 1024),
        cost_estimate=pl.CostEstimate(flops=16 * 48 * 256, bytes_accessed=442368, transcendentals=0),
        name="plane_sums",
    )(terms)


def block_integrals(picked):
    side = AW * BLOCK_VIRTUALS
    return pl.pallas_call(
        integrals_kernel,
        out_shape=jax.ShapeDtypeStruct((GROUP, AW, QUARTER + LANES), jnp.float32),
        in_specs=[pl.BlockSpec(memory_space=pltpu.VMEM)],
        out_specs=pl.BlockSpec(memory_space=pltpu.VMEM),
        scratch_shapes=[
            pltpu.VMEM((side, side), jnp.bfloat16),
            pltpu.VMEM((side, side), jnp.bfloat16),
            pltpu.VMEM((AW, BLOCK_VIRTUALS, side), jnp.float32),
        ],
        compiler_params=pltpu.CompilerParams(vmem_limit_bytes=24 * 1024 * 1024),
        cost_estimate=pl.CostEstimate(
            flops=2 * side**3, bytes_accessed=2 * 1024 * 1024, transcendentals=0
        ),
        name="block_integrals",
    )(picked)


def table_lookup(index_list, table):
    slots_here = jnp.arange(table.shape[0], dtype=jnp.int32)
    return jnp.sum(
        jnp.where(index_list[:, None] == slots_here[None, :], table[None, :], 0.0), axis=1
    )


def one_hot_rows(columns, width):
    cols = lax.broadcasted_iota(jnp.int32, (columns.shape[0], width), 1)
    return (columns[:, None] == cols).astype(jnp.bfloat16)


def select_rows(hot, rows):
    return lax.dot_general(
        hot, rows, (((1,), (1,)), ((), ())), preferred_element_type=jnp.float32
    ).astype(jnp.bfloat16)


def shards(
    factor, amplitude_forward, amplitude_reversed, block_map, pair_list, virt_energy, occ_energy
):
    plane_map = lax.all_to_all(
        jnp.broadcast_to(block_map, (16, 2)), PLANE, 0, 0, tiled=True
    )
    line = lax.all_gather(factor, "z", axis=0, tiled=True)
    q_line = line.shape[0]
    wanted = (
        plane_map.reshape(-1, 1) * BLOCK_VIRTUALS + jnp.arange(BLOCK_VIRTUALS, dtype=jnp.int32)
    ).reshape(-1)
    line = line.transpose(1, 0, 2).reshape(AW * q_line, NV)
    picked = select_rows(one_hot_rows(wanted, NV), line)
    picked = picked.reshape(16, 2 * BLOCK_VIRTUALS, AW * q_line)
    picked = lax.all_to_all(picked, PLANE, 0, 0, tiled=True)
    partial_sum = block_integrals(picked).astype(jnp.float16)
    quarters = lax.all_to_all(partial_sum, "yh", 0, 0, tiled=True)
    quarters = quarters.astype(jnp.float32)
    unscale = jnp.exp2(quarters[:, :1, QUARTER : QUARTER + 1] - TOP)
    coulomb = jnp.sum(quarters[:, :, :QUARTER] * unscale, axis=0)
    gathered = lax.all_gather(coulomb.astype(jnp.bfloat16), "yh", axis=0, tiled=True)
    ordered = residual_terms(amplitude_forward, amplitude_reversed, gathered)
    ordered = lax.all_to_all(ordered, PLANE, 0, 0, tiled=True)
    plane_sum = plane_sums(ordered)
    owned = jnp.sum(lax.all_to_all(plane_sum, "z", 0, 0, tiled=True), axis=0)

    owned_len = owned.shape[1]
    offset = lax.axis_index(BLK) * owned_len
    flat_index = offset + jnp.arange(owned_len, dtype=jnp.int32)
    pair_at = flat_index // (AW * AW)
    cell_index = flat_index % (AW * AW)
    pair_energy = table_lookup(pair_list[:, 0], occ_energy) + table_lookup(
        pair_list[:, 1], occ_energy
    )
    owned_pair = table_lookup(pair_at, pair_energy)
    energy_a = table_lookup(cell_index // AW, virt_energy)
    energy_b = table_lookup(cell_index % AW, virt_energy)
    denominator = owned_pair - energy_a - energy_b
    return owned / denominator.reshape(1, owned_len)


def solution(mesh):
    fine = Mesh(mesh.devices.reshape(2, 4, 16, 2, 4), BLK + ("yh",))
    placed = (
        P(BLK + ("yh",), None, None),
        P(BLK, "yh", None),
        P(BLK, "yh", None),
        P(BLK, None),
        P("yh", None),
        P(),
        P(),
    )
    return jax.shard_map(
        shards, mesh=fine, in_specs=placed, out_specs=P("yh", BLK), check_vma=False
    )
```

```python
import jax
import jax.numpy as jnp
from jax import lax
from jax.experimental import pallas as pl
from jax.experimental.pallas import tpu as pltpu
from jax.sharding import Mesh
from jax.sharding import PartitionSpec as P

AW = 16
BLOCK_VIRTUALS = 32
NV = 704
BLK = ("yl", "x", "z", "core")
PLANE = ("yl", "x", "core")
SPREAD = ("x", "yl", "core")
GROUP = 4
LANES = 128
PAIRS = BLOCK_VIRTUALS**2
TOP = 14.0
QUARTER = GROUP * PAIRS


def swap_lane_blocks(tiles):
    lane = lax.broadcasted_iota(jnp.int32, tiles[0].shape, 1)
    block = lax.shift_right_logical(lane, 5)
    result = []
    for j in range(GROUP):
        out = None
        for i in range(GROUP):
            shift = (i - j) * BLOCK_VIRTUALS % LANES
            moved = pltpu.roll(tiles[i], shift, 1) if shift else tiles[i]
            out = moved if out is None else jnp.where(block == i, moved, out)
        result.append(out)
    return result


def integrals_kernel(picked_ref, out_ref, left_ref, right_ref, product_ref):
    for source in range(0, 16, GROUP):
        for first in range(0, AW, GROUP):
            lanes = slice(first * BLOCK_VIRTUALS, first * BLOCK_VIRTUALS + LANES)
            tiles = [
                picked_ref[source + i, :, lanes].astype(jnp.float32) for i in range(GROUP)
            ]
            depth = slice(source * BLOCK_VIRTUALS, source * BLOCK_VIRTUALS + LANES)
            for j, tile in enumerate(swap_lane_blocks(tiles)):
                rows = slice((first + j) * BLOCK_VIRTUALS, (first + j + 1) * BLOCK_VIRTUALS)
                tile = tile.astype(jnp.bfloat16)
                left_ref[rows, depth] = tile[:BLOCK_VIRTUALS]
                right_ref[rows, depth] = tile[BLOCK_VIRTUALS:]
    product = lax.dot_general(
        left_ref[...],
        right_ref[...],
        (((1,), (1,)), ((), ())),
        preferred_element_type=jnp.float32,
    )
    largest = jnp.max(jnp.max(jnp.abs(product), axis=0, keepdims=True), axis=1, keepdims=True)
    power = jnp.ceil(jnp.log2(jnp.maximum(largest, 2.0**-100)))
    scale = jnp.exp2(TOP - power)
    product_ref[...] = (product * scale).reshape(product_ref.shape)
    out_ref[:, :, QUARTER:] = jnp.broadcast_to(power, (GROUP * AW, LANES)).reshape(GROUP, AW, LANES)
    for c in range(0, BLOCK_VIRTUALS, GROUP):
        for b in range(0, AW, GROUP):
            lanes = slice(b * BLOCK_VIRTUALS, b * BLOCK_VIRTUALS + LANES)
            tiles = [product_ref[:, c + i, lanes] for i in range(GROUP)]
            for j, tile in enumerate(swap_lane_blocks(tiles)):
                at = j * PAIRS + c * BLOCK_VIRTUALS
                out_ref[b // GROUP, :, at : at + LANES] = tile


def select_matmul(hot, rows):
    return jnp.dot(hot, rows, preferred_element_type=jnp.float32).astype(jnp.bfloat16)


def residual_kernel(forward_ref, reversed_ref, gathered_ref, out_ref, term_ref, mirrored_ref):
    for b in range(AW):
        rows = slice(b // GROUP * AW, (b // GROUP + 1) * AW)
        lanes = slice(b % GROUP * PAIRS, (b % GROUP + 1) * PAIRS)
        mirrored_ref[b * AW : (b + 1) * AW] = gathered_ref[rows, lanes]
    cells = AW * AW
    row = lax.broadcasted_iota(jnp.int32, (cells, cells), 0)
    col = lax.broadcasted_iota(jnp.int32, (cells, cells), 1)
    other = lax.bitwise_and(row, AW - 1) * AW + lax.shift_right_logical(row, 4)
    hot = (col == other).astype(jnp.bfloat16)
    weights = select_matmul(hot, mirrored_ref[...])
    across = (((1,), (1,)), ((), ()))
    term_ref[...] = (
        lax.dot_general(
            forward_ref[0], weights, across, preferred_element_type=jnp.float32
        )
        + lax.dot_general(
            reversed_ref[0], mirrored_ref[...], across, preferred_element_type=jnp.float32
        )
    ).astype(jnp.bfloat16)
    piece = 96
    row = lax.broadcasted_iota(jnp.int32, (piece, piece), 0)
    col = lax.broadcasted_iota(jnp.int32, (piece, piece), 1)
    core = (row >= piece // 2).astype(jnp.int32)
    within = row - core * (piece // 2)
    line = lax.shift_right_logical(within * 171, 9)
    hot = (col == line * 3 + within + core * 3).astype(jnp.bfloat16)
    for at in range(8):
        ordered = select_matmul(hot, term_ref[at * piece : (at + 1) * piece])
        out_ref[at * 2] = ordered[: piece // 2]
        out_ref[at * 2 + 1] = ordered[piece // 2 :]


def residual_terms(forward, backward, gathered):
    return pl.pallas_call(
        residual_kernel,
        out_shape=jax.ShapeDtypeStruct((16, 48, AW * AW), jnp.bfloat16),
        in_specs=[pl.BlockSpec(memory_space=pltpu.VMEM)] * 3,
        out_specs=pl.BlockSpec(memory_space=pltpu.VMEM),
        scratch_shapes=[
            pltpu.VMEM((768, AW * AW), jnp.bfloat16),
            pltpu.VMEM((AW * AW, PAIRS), jnp.bfloat16),
        ],
        compiler_params=pltpu.CompilerParams(vmem_limit_bytes=24 * 1024 * 1024),
        cost_estimate=pl.CostEstimate(
            flops=4 * 768 * 256 * 1024, bytes_accessed=4 * 1024 * 1024, transcendentals=0
        ),
        name="residual_terms",
    )(forward, backward, gathered)


def plane_sum_kernel(terms_ref, out_ref, total_ref):
    total = terms_ref[0].astype(jnp.float32)
    for source in range(1, 16):
        total = total + terms_ref[source].astype(jnp.float32)
    total_ref[...] = total
    cells = AW * AW
    for z in range(16):
        for k in range(3):
            out_ref[z, :, k * cells : (k + 1) * cells] = total_ref[z * 3 + k : z * 3 + k + 1]


def plane_sums(terms):
    return pl.pallas_call(
        plane_sum_kernel,
        out_shape=jax.ShapeDtypeStruct((16, 1, 768), jnp.float32),
        in_specs=[pl.BlockSpec(memory_space=pltpu.VMEM)],
        out_specs=pl.BlockSpec(memory_space=pltpu.VMEM),
        scratch_shapes=[pltpu.VMEM((48, AW * AW), jnp.float32)],
        compiler_params=pltpu.CompilerParams(vmem_limit_bytes=8 * 1024 * 1024),
        cost_estimate=pl.CostEstimate(flops=16 * 48 * 256, bytes_accessed=442368, transcendentals=0),
        name="plane_sums",
    )(terms)


def block_integrals(picked):
    side = AW * BLOCK_VIRTUALS
    return pl.pallas_call(
        integrals_kernel,
        out_shape=jax.ShapeDtypeStruct((GROUP, AW, QUARTER + LANES), jnp.float32),
        in_specs=[pl.BlockSpec(memory_space=pltpu.VMEM)],
        out_specs=pl.BlockSpec(memory_space=pltpu.VMEM),
        scratch_shapes=[
            pltpu.VMEM((side, side), jnp.bfloat16),
            pltpu.VMEM((side, side), jnp.bfloat16),
            pltpu.VMEM((AW, BLOCK_VIRTUALS, side), jnp.float32),
        ],
        compiler_params=pltpu.CompilerParams(vmem_limit_bytes=24 * 1024 * 1024),
        cost_estimate=pl.CostEstimate(
            flops=2 * side**3, bytes_accessed=2 * 1024 * 1024, transcendentals=0
        ),
        name="block_integrals",
    )(picked)


def table_lookup(index_list, table):
    slots_here = jnp.arange(table.shape[0], dtype=jnp.int32)
    return jnp.sum(
        jnp.where(index_list[:, None] == slots_here[None, :], table[None, :], 0.0), axis=1
    )


def one_hot_rows(columns, width):
    cols = lax.broadcasted_iota(jnp.int32, (columns.shape[0], width), 1)
    return (columns[:, None] == cols).astype(jnp.bfloat16)


def select_rows(hot, rows):
    return lax.dot_general(
        hot, rows, (((1,), (1,)), ((), ())), preferred_element_type=jnp.float32
    ).astype(jnp.bfloat16)


def shards(
    factor, amplitude_forward, amplitude_reversed, block_map, pair_list, virt_energy, occ_energy
):
    plane_map = lax.all_to_all(
        jnp.broadcast_to(block_map, (16, 2)), SPREAD, 0, 0, tiled=True
    )
    line = lax.all_gather(factor, "z", axis=0, tiled=True)
    q_line = line.shape[0]
    wanted = (
        plane_map.reshape(-1, 1) * BLOCK_VIRTUALS + jnp.arange(BLOCK_VIRTUALS, dtype=jnp.int32)
    ).reshape(-1)
    line = line.transpose(1, 0, 2).reshape(AW * q_line, NV)
    picked = select_rows(one_hot_rows(wanted, NV), line)
    picked = picked.reshape(16, 2 * BLOCK_VIRTUALS, AW * q_line)
    picked = lax.all_to_all(picked, SPREAD, 0, 0, tiled=True)
    partial_sum = block_integrals(picked).astype(jnp.float16)
    quarters = lax.all_to_all(partial_sum, "yh", 0, 0, tiled=True)
    quarters = quarters.astype(jnp.float32)
    unscale = jnp.exp2(quarters[:, :1, QUARTER : QUARTER + 1] - TOP)
    coulomb = jnp.sum(quarters[:, :, :QUARTER] * unscale, axis=0)
    gathered = lax.all_gather(coulomb.astype(jnp.bfloat16), "yh", axis=0, tiled=True)
    ordered = residual_terms(amplitude_forward, amplitude_reversed, gathered)
    ordered = lax.all_to_all(ordered, PLANE, 0, 0, tiled=True)
    plane_sum = plane_sums(ordered)
    owned = jnp.sum(lax.all_to_all(plane_sum, "z", 0, 0, tiled=True), axis=0)

    owned_len = owned.shape[1]
    offset = lax.axis_index(BLK) * owned_len
    flat_index = offset + jnp.arange(owned_len, dtype=jnp.int32)
    pair_at = flat_index // (AW * AW)
    cell_index = flat_index % (AW * AW)
    pair_energy = table_lookup(pair_list[:, 0], occ_energy) + table_lookup(
        pair_list[:, 1], occ_energy
    )
    owned_pair = table_lookup(pair_at, pair_energy)
    energy_a = table_lookup(cell_index // AW, virt_energy)
    energy_b = table_lookup(cell_index % AW, virt_energy)
    denominator = owned_pair - energy_a - energy_b
    return owned / denominator.reshape(1, owned_len)


def solution(mesh):
    fine = Mesh(mesh.devices.reshape(2, 4, 16, 2, 4), BLK + ("yh",))
    placed = (
        P(BLK + ("yh",), None, None),
        P(BLK, "yh", None),
        P(BLK, "yh", None),
        P(BLK, None),
        P("yh", None),
        P(),
        P(),
    )
    return jax.shard_map(
        shards, mesh=fine, in_specs=placed, out_specs=P("yh", BLK), check_vma=False
    )
```
